512 devices in a mesh: space: 32 (over z, y_hi), field: 16 (over y_lo, x, core).
Axes of the slice: x: 4, y: 8 (y_hi: 4, y_lo: 2; y = y_hi * 2 + y_lo), z: 8, core: 2. Of those that a mesh axis runs over, the one named last changes fastest.
Arguments:
- phi: float32 [16, 8, 96, 48, 128], P('field', None, 'space'), may hold values from -6 to 6
- velocity: float32 [3, 96, 48, 128], P(None, 'space'), may hold values from -1 to 1
- wiener: float32 [16, 3, 96, 48, 128], P('field', None, 'space'), may hold values from -3 to 3
- diffusivity: float32 [96, 48, 128], P('space'), may hold values from 0.02 to 0.1
- stoich: float32 [8], replicated, may hold values from -1 to 1
Outputs:
- phi_next: float32 [16, 8, 96, 48, 128], P('field', None, 'space')
The draws below stay inside these ranges and needn't reach their ends.
All inputs are finite; a program needn't handle non-finite values.
Results may differ from the reference program's by a relative error of at most 0.00002.
Values sent between devices are 32-bit elements; how exact they have to be, the bound alone decides.
No kernel may reach another device: no remote copies, remote signals or barrier semaphores. Data moves between devices by JAX's collectives and lax.ppermute only.
A program may use at most 64 MiB of HBM per device.

```python
import math
import jax
import jax.numpy as jnp
from jax import lax

S = 8
NY = 48
NZ = 128
FIELDS = 16
NX = 96


def block_scale(rng, shape, split, smallest, top_value):
    factor_of, own = 1.0, jax.random.fold_in(rng, 6)
    for position, shards_of in split:
        steps = jnp.exp(jax.random.uniform(jax.random.fold_in(own, position), (shards_of,), jnp.float32, smallest / len(split), top_value / len(split)))
        factor_of = factor_of * jnp.repeat(steps, shape[position] // shards_of).reshape([-1 if axis == position else 1 for axis in range(len(shape))])
    return factor_of


def scatter_about(stream_key, shape, width, limit, cuts=(), dtype=jnp.bfloat16):
    gain = block_scale(stream_key, shape, cuts, -0.22, 0.18) if cuts else 1.0
    drawn = jax.random.normal(stream_key, shape, jnp.float32) * width * gain
    return jnp.minimum(jnp.maximum(drawn, -limit), limit).astype(dtype)


def setup_inputs(seed: int = 0) -> dict:
    key_of = jax.random.split(jax.random.key(seed), 6)
    return {
        "phi": scatter_about(key_of[0], (FIELDS, S, NX, NY, NZ), 1.0, 6.0, ((0, 16), (2, 32)), jnp.float32),
        "velocity": jnp.clip(jax.random.uniform(key_of[1], (3, NX, NY, NZ), jnp.float32, -1.0, 1.0) * block_scale(key_of[1], (3, NX, NY, NZ), ((1, 32),), -0.4, 0.0), -1.0, 1.0),
        "wiener": scatter_about(key_of[2], (FIELDS, 3, NX, NY, NZ), 0.5, 3.0, ((0, 16), (2, 32)), jnp.float32),
        "diffusivity": jnp.clip(jnp.exp(math.log(0.1) - 1.609438 * jax.random.uniform(key_of[3], (NX, NY, NZ), jnp.float32) ** block_scale(key_of[3], (NX, NY, NZ), ((0, 32),), -0.2, 0.2)), 0.02, 0.1),
        "stoich": jnp.clip(jax.random.uniform(key_of[4], (S,), jnp.float32, -1.0, 1.0), -1.0, 1.0),
    }


time_step = 0.3
mix_const = 5.0
pre_factor = 2.0
activation = 2.0

def stencil(padded, num_cells):

    def along_x(k):
        return padded[:, 3 + k:3 + k + num_cells]
    centre = along_x(0)

    def along_y(k):
        return jnp.roll(centre, -k, axis=2)

    def along_z(k):
        return jnp.roll(centre, -k, axis=3)

    def derivative(g):
        return (45.0 * (g(1) - g(-1)) - 9.0 * (g(2) - g(-2)) + (g(3) - g(-3))) / 60.0
    laplace = along_x(1) + along_x(-1) + along_y(1) + along_y(-1) + along_z(1) + along_z(-1) - 6.0 * centre
    return (centre, derivative(along_x), derivative(along_y), derivative(along_z), laplace)

def increment(padded, velocity, wiener, diffusion, field_mean, amplitude, stoich):
    centre, grad_x, grad_y, grad_z, laplace = stencil(padded, velocity.shape[1])
    advect = -(velocity[0] * grad_x + velocity[1] * grad_y + velocity[2] * grad_z)
    noise_term = amplitude * (wiener[0] * grad_x + wiener[1] * grad_y + wiener[2] * grad_z)
    mixing = -mix_const * diffusion * (centre - field_mean)
    theta_cell = 1.0 + 3.0 * jax.nn.sigmoid(centre[7])
    arrhenius = pre_factor * centre[0] * centre[1] * jnp.exp(-activation / theta_cell)
    reaction = stoich[:, None, None, None] * arrhenius
    return centre + time_step * (advect + diffusion * laplace + mixing + reaction) + noise_term

def reference(phi, velocity, wiener, diffusivity, stoich):

    def advance(state):
        field_mean = lax.optimization_barrier(jnp.sum(state, axis=0)) / FIELDS
        amplitude = jnp.sqrt(2.0 * diffusivity * (1.0 + 3.0 * jax.nn.sigmoid(field_mean[7])))

        def single(pair):
            padded = jnp.pad(pair[0], ((0, 0), (3, 3), (0, 0), (0, 0)))
            return increment(padded, velocity, pair[1], diffusivity, field_mean, amplitude, stoich)
        return lax.map(single, (state, wiener))
    first = advance(phi)
    second = advance(first)
    return 0.5 * phi + 0.5 * second
```

```python
import functools

import jax
import jax.numpy as jnp
from jax import lax
from jax.experimental import pallas as pl
from jax.experimental.pallas import tpu as pltpu
from jax.sharding import PartitionSpec as P

time_step = 0.3
mix_const = 5.0
pre_factor = 2.0
activation = 2.0


def sigmoid(x):
    return 1.0 / (1.0 + jnp.exp(-x))


def section_kernel(fields, last, stoich_ref, q_ref, low_ref, high_ref, vel_ref, wie_ref, dif_ref, sum_ref, *rest):
    if last:
        base_ref, out_ref, coef, react = rest
    else:
        out_ref, coef, react = rest
    scalars, planes = q_ref.shape[:2]

    for i in range(planes):
        dif = dif_ref[i]
        theta_bar = 1.0 + 3.0 * sigmoid(sum_ref[scalars - 1, i] / fields)
        amplitude = jnp.sqrt(2.0 * dif * theta_bar)
        for d in range(3):
            coef[d, i] = amplitude * wie_ref[d, i] - time_step * vel_ref[d, i]
        theta = 1.0 + 3.0 * sigmoid(q_ref[scalars - 1, i])
        react[i] = (time_step * pre_factor) * q_ref[0, i] * q_ref[1, i] * jnp.exp(-activation / theta)

    def one(s, carry):
        for i in range(planes):

            def along_x(k):
                j = i + k
                if j < 0:
                    return low_ref[s, j + planes]
                if j >= planes:
                    return high_ref[s, j - planes]
                return q_ref[s, j]

            q = q_ref[s, i]
            rows, lanes = q.shape
            near = None
            grown = None
            for d in range(3):
                if d == 0:
                    at = along_x
                else:
                    size = (rows, lanes)[d - 1]
                    at = lambda k, d=d, size=size: pltpu.roll(q, (-k) % size, d - 1)
                up, down = at(1), at(-1)
                slope = 0.75 * (up - down) - 0.15 * (at(2) - at(-2)) + (1.0 / 60.0) * (at(3) - at(-3))
                term = coef[d, i] * slope
                pair = up + down
                near = pair if near is None else near + pair
                grown = term if grown is None else grown + term
            smooth = near - 6.0 * q - mix_const * (q - sum_ref[s, i] * (1.0 / fields))
            new = q + (grown + time_step * dif_ref[i] * smooth + stoich_ref[s] * react[i])
            if last:
                new = 0.5 * base_ref[s, i] + 0.5 * new
            out_ref[s, i] = new
        return carry

    lax.fori_loop(0, scalars, one, 0)


def section(fields, stoich, q, low, high, velocity, wiener, diffusivity, total, base=None):
    last = base is not None
    planes, rows, lanes = q.shape[1:]
    vmem = pl.BlockSpec(memory_space=pltpu.VMEM)
    args = (q, low, high, velocity, wiener, diffusivity, total) + ((base,) if last else ())
    return pl.pallas_call(
        functools.partial(section_kernel, fields, last),
        out_shape=jax.ShapeDtypeStruct(q.shape, q.dtype),
        in_specs=[pl.BlockSpec(memory_space=pltpu.SMEM)] + [vmem] * len(args),
        out_specs=vmem,
        scratch_shapes=[
            pltpu.VMEM((3, planes, rows, lanes), jnp.float32),
            pltpu.VMEM((planes, rows, lanes), jnp.float32),
        ],
        compiler_params=pltpu.CompilerParams(vmem_limit_bytes=16 * 2**20),
        cost_estimate=pl.CostEstimate(flops=80 * q.size, bytes_accessed=24 * q.size, transcendentals=q.size // 8),
        name="section_last" if last else "section_first",
    )(stoich, *args)


def field_sum(q):
    count = lax.axis_size("field")
    shares = q.reshape(count, -1, 8, q.shape[-1])
    share = jnp.sum(lax.all_to_all(shares, "field", 0, 0), axis=0)
    whole = lax.all_to_all(jnp.broadcast_to(share, shares.shape), "field", 0, 0)
    return whole.reshape(q.shape)


def neighbours(q):
    count = lax.axis_size("space")
    low = lax.ppermute(q, "space", [(i, i + 1) for i in range(count - 1)])
    high = lax.ppermute(q, "space", [(i + 1, i) for i in range(count - 1)])
    return low, high


def local(phi, velocity, wiener, diffusivity, stoich):
    fields = phi.shape[0] * lax.axis_size("field")
    phi, wiener = phi[0], wiener[0]
    low, high = neighbours(phi)
    first = section(fields, stoich, phi, low, high, velocity, wiener, diffusivity, field_sum(phi))
    low, high = neighbours(first)
    out = section(fields, stoich, first, low, high, velocity, wiener, diffusivity, field_sum(first), phi)
    return out[None]


def solution(mesh):
    return jax.shard_map(
        local,
        mesh=mesh,
        in_specs=(
            P("field", None, "space", None, None),
            P(None, "space", None, None),
            P("field", None, "space", None, None),
            P("space", None, None),
            P(),
        ),
        out_specs=P("field", None, "space", None, None),
        check_vma=False,
    )
```

```python
import functools

import jax
import jax.numpy as jnp
from jax import lax
from jax.experimental import pallas as pl
from jax.experimental.pallas import tpu as pltpu
from jax.sharding import PartitionSpec as P

time_step = 0.3
mix_const = 5.0
pre_factor = 2.0
activation = 2.0


def sigmoid(x):
    return 1.0 / (1.0 + jnp.exp(-x))


def section_kernel(fields, last, stoich_ref, q_ref, low_a, low_b, high_a, high_b, vel_ref, wie_ref, dif_ref, sum_ref, *rest):
    if last:
        base_ref, out_ref, coef, react = rest
    else:
        out_ref, coef, react = rest
    scalars, planes = q_ref.shape[:2]

    for i in range(planes):
        dif = dif_ref[i]
        theta_bar = 1.0 + 3.0 * sigmoid(sum_ref[scalars - 1, i] / fields)
        amplitude = jnp.sqrt(2.0 * dif * theta_bar)
        for d in range(3):
            coef[d, i] = amplitude * wie_ref[d, i] - time_step * vel_ref[d, i]
        theta = 1.0 + 3.0 * sigmoid(q_ref[scalars - 1, i])
        react[i] = (time_step * pre_factor) * q_ref[0, i] * q_ref[1, i] * jnp.exp(-activation / theta)

    half = scalars // 2

    def one(low_ref, high_ref, first, n, carry):
        s = first + n
        for i in range(planes):

            def along_x(k):
                j = i + k
                if j < 0:
                    return low_ref[n, j + planes]
                if j >= planes:
                    return high_ref[n, j - planes]
                return q_ref[s, j]

            q = q_ref[s, i]
            rows, lanes = q.shape
            near = None
            grown = None
            for d in range(3):
                if d == 0:
                    at = along_x
                else:
                    size = (rows, lanes)[d - 1]
                    at = lambda k, d=d, size=size: pltpu.roll(q, (-k) % size, d - 1)
                up, down = at(1), at(-1)
                slope = 0.75 * (up - down) - 0.15 * (at(2) - at(-2)) + (1.0 / 60.0) * (at(3) - at(-3))
                term = coef[d, i] * slope
                pair = up + down
                near = pair if near is None else near + pair
                grown = term if grown is None else grown + term
            smooth = near - 6.0 * q - mix_const * (q - sum_ref[s, i] * (1.0 / fields))
            new = q + (grown + time_step * dif_ref[i] * smooth + stoich_ref[s] * react[i])
            if last:
                new = 0.5 * base_ref[s, i] + 0.5 * new
            out_ref[s, i] = new
        return carry

    lax.fori_loop(0, half, functools.partial(one, low_a, high_a, 0), 0)
    lax.fori_loop(0, half, functools.partial(one, low_b, high_b, half), 0)


def section(fields, stoich, q, halo, velocity, wiener, diffusivity, total, base=None):
    last = base is not None
    planes, rows, lanes = q.shape[1:]
    vmem = pl.BlockSpec(memory_space=pltpu.VMEM)
    args = (q, *halo, velocity, wiener, diffusivity, total) + ((base,) if last else ())
    return pl.pallas_call(
        functools.partial(section_kernel, fields, last),
        out_shape=jax.ShapeDtypeStruct(q.shape, q.dtype),
        in_specs=[pl.BlockSpec(memory_space=pltpu.SMEM)] + [vmem] * len(args),
        out_specs=vmem,
        scratch_shapes=[
            pltpu.VMEM((3, planes, rows, lanes), jnp.float32),
            pltpu.VMEM((planes, rows, lanes), jnp.float32),
        ],
        compiler_params=pltpu.CompilerParams(vmem_limit_bytes=16 * 2**20),
        cost_estimate=pl.CostEstimate(flops=80 * q.size, bytes_accessed=24 * q.size, transcendentals=q.size // 8),
        name="section_last" if last else "section_first",
    )(stoich, *args)


def neighbours(q):
    count = lax.axis_size("space")
    low = lax.ppermute(q, "space", [(i, i + 1) for i in range(count - 1)])
    high = lax.ppermute(q, "space", [(i + 1, i) for i in range(count - 1)])
    return low, high


def exchange(q):
    count = lax.axis_size("field")
    half = q.shape[0] // 2
    shares = q.reshape(count, -1, 8, q.shape[-1])
    low_a, high_a = neighbours(q[:half])
    share = jnp.sum(lax.all_to_all(shares, "field", 0, 0), axis=0)
    share, low_a, high_a, rest = lax.optimization_barrier((share, low_a, high_a, q[half:]))
    low_b, high_b = neighbours(rest)
    whole = lax.all_to_all(jnp.broadcast_to(share, shares.shape), "field", 0, 0)
    return whole.reshape(q.shape), (low_a, low_b, high_a, high_b)


def local(phi, velocity, wiener, diffusivity, stoich):
    fields = phi.shape[0] * lax.axis_size("field")
    phi, wiener = phi[0], wiener[0]
    total, halo = exchange(phi)
    first = section(fields, stoich, phi, halo, velocity, wiener, diffusivity, total)
    total, halo = exchange(first)
    out = section(fields, stoich, first, halo, velocity, wiener, diffusivity, total, phi)
    return out[None]


def solution(mesh):
    return jax.shard_map(
        local,
        mesh=mesh,
        in_specs=(
            P("field", None, "space", None, None),
            P(None, "space", None, None),
            P("field", None, "space", None, None),
            P("space", None, None),
            P(),
        ),
        out_specs=P("field", None, "space", None, None),
        check_vma=False,
    )
```

```python
import functools

import jax
import jax.numpy as jnp
from jax import lax
from jax.experimental import pallas as pl
from jax.experimental.pallas import tpu as pltpu
from jax.sharding import PartitionSpec as P

time_step = 0.3
mix_const = 5.0
pre_factor = 2.0
activation = 2.0

SMEM = pl.BlockSpec(memory_space=pltpu.SMEM)
VMEM = pl.BlockSpec(memory_space=pltpu.VMEM)


def call(kernel, out_shape, in_specs, scratch, flops, name):
    return pl.pallas_call(
        kernel,
        out_shape=out_shape,
        in_specs=in_specs,
        out_specs=jax.tree.map(lambda _: VMEM, out_shape),
        scratch_shapes=scratch,
        compiler_params=pltpu.CompilerParams(vmem_limit_bytes=16 * 2**20),
        cost_estimate=pl.CostEstimate(flops=flops, bytes_accessed=0, transcendentals=0),
        name=name,
    )


def sigmoid(x):
    return 1.0 / (1.0 + jnp.exp(-x))


def parts_kernel(stoich_ref, q_ref, low_ref, high_ref, vel_ref, wie_ref, dif_ref, base_ref, noise_ref, react):
    scalars, planes = q_ref.shape[:2]
    for i in range(planes):
        theta = 1.0 + 3.0 * sigmoid(q_ref[scalars - 1, i])
        react[i] = (time_step * pre_factor) * q_ref[0, i] * q_ref[1, i] * jnp.exp(-activation / theta)

    def one(s, carry):
        for i in range(planes):

            def along_x(k):
                j = i + k
                if j < 0:
                    return low_ref[s, j + planes]
                if j >= planes:
                    return high_ref[s, j - planes]
                return q_ref[s, j]

            q = q_ref[s, i]
            rows, lanes = q.shape
            near = None
            for d in range(3):
                if d == 0:
                    at = along_x
                else:
                    size = (rows, lanes)[d - 1]
                    at = lambda k, d=d, size=size: pltpu.roll(q, (-k) % size, d - 1)
                up, down = at(1), at(-1)
                slope = 0.75 * (up - down) - 0.15 * (at(2) - at(-2)) + (1.0 / 60.0) * (at(3) - at(-3))
                drift = vel_ref[d, i] * slope
                shake = wie_ref[d, i] * slope
                pair = up + down
                near, drifts, shakes = (pair, drift, shake) if near is None else (near + pair, drifts + drift, shakes + shake)
            smooth = dif_ref[i] * (near - (6.0 + mix_const) * q)
            base_ref[s, i] = q + (time_step * (smooth - drifts) + stoich_ref[s] * react[i])
            noise_ref[s, i] = shakes
        return carry

    lax.fori_loop(0, scalars, one, 0)


def join_kernel(fields, last, base_ref, noise_ref, dif_ref, total_ref, *rest):
    out_ref = rest[-1]
    scalars, planes = base_ref.shape[:2]
    for i in range(planes):
        dif = dif_ref[i]
        theta_bar = 1.0 + 3.0 * sigmoid(total_ref[scalars - 1, i] * (1.0 / fields))
        amplitude = jnp.sqrt(2.0 * dif * theta_bar)
        pull = (time_step * mix_const / fields) * dif
        for s in range(scalars):
            new = base_ref[s, i] + (amplitude * noise_ref[s, i] + pull * total_ref[s, i])
            out_ref[s, i] = 0.5 * rest[0][s, i] + 0.5 * new if last else new


def spread_kernel(parts_ref, out_ref):
    count = parts_ref.shape[0]
    total = parts_ref[0]
    for n in range(1, count):
        total = total + parts_ref[n]
    for n in range(count):
        out_ref[n] = total


def section(fields, stoich, q, velocity, wiener, diffusivity, base=None):
    last = base is not None
    field_count = lax.axis_size("field")
    like = jax.ShapeDtypeStruct(q.shape, q.dtype)
    shares = q.reshape(field_count, -1, 8, q.shape[-1])
    received = lax.all_to_all(shares, "field", 0, 0)
    low, high = neighbours(q)
    spread = call(spread_kernel, jax.ShapeDtypeStruct(shares.shape, q.dtype), [VMEM], [], 0, "spread")(received)
    total = lax.all_to_all(spread, "field", 0, 0).reshape(q.shape)
    drift, noise = call(
        parts_kernel, (like, like), [SMEM] + [VMEM] * 6, [pltpu.VMEM(q.shape[1:], jnp.float32)], 10**10, "parts"
    )(stoich, q, low, high, velocity, wiener, diffusivity)
    args = (drift, noise, diffusivity, total) + ((base,) if last else ())
    return call(functools.partial(join_kernel, fields, last), like, [VMEM] * len(args), [], 0, "join")(*args)


def neighbours(q):
    count = lax.axis_size("space")
    low = lax.ppermute(q, "space", [(i, i + 1) for i in range(count - 1)])
    high = lax.ppermute(q, "space", [(i + 1, i) for i in range(count - 1)])
    return low, high


def local(phi, velocity, wiener, diffusivity, stoich):
    fields = phi.shape[0] * lax.axis_size("field")
    phi, wiener = phi[0], wiener[0]
    first = section(fields, stoich, phi, velocity, wiener, diffusivity)
    return section(fields, stoich, first, velocity, wiener, diffusivity, phi)[None]


def solution(mesh):
    return jax.shard_map(
        local,
        mesh=mesh,
        in_specs=(
            P("field", None, "space", None, None),
            P(None, "space", None, None),
            P("field", None, "space", None, None),
            P("space", None, None),
            P(),
        ),
        out_specs=P("field", None, "space", None, None),
        check_vma=False,
    )
```

```python
import functools

import jax
import jax.numpy as jnp
from jax import lax
from jax.experimental import pallas as pl
from jax.experimental.pallas import tpu as pltpu
from jax.sharding import PartitionSpec as P

time_step = 0.3
mix_const = 5.0
pre_factor = 2.0
activation = 2.0

HBM = pl.BlockSpec(memory_space=pltpu.HBM)
SMEM = pl.BlockSpec(memory_space=pltpu.SMEM)
VMEM = pl.BlockSpec(memory_space=pltpu.VMEM)


FIELD_ROWS = [[(y * 4 + x) * 2 + c for x in range(4) for c in range(2)] for y in range(2)]


def call(kernel, out_shape, in_specs, scratch, flops, name, aliases={}):
    return pl.pallas_call(
        kernel,
        out_shape=out_shape,
        in_specs=in_specs,
        out_specs=jax.tree.map(lambda _: VMEM, out_shape),
        scratch_shapes=scratch,
        compiler_params=pltpu.CompilerParams(vmem_limit_bytes=16 * 2**20),
        cost_estimate=pl.CostEstimate(flops=flops, bytes_accessed=0, transcendentals=0),
        input_output_aliases=aliases,
        name=name,
    )


def sigmoid(x):
    return 1.0 / (1.0 + jnp.exp(-x))


def slope_of(at):
    up, down = at(1), at(-1)
    return 0.75 * (up - down) - 0.15 * (at(2) - at(-2)) + (1.0 / 60.0) * (at(3) - at(-3)), up + down


def inner_kernel(stoich_ref, q_ref, vel_ref, wie_ref, dif_ref, base_ref, noise_ref, react):
    scalars, planes = q_ref.shape[:2]
    for i in range(planes):
        theta = 1.0 + 3.0 * sigmoid(q_ref[scalars - 1, i])
        react[i] = (time_step * pre_factor) * q_ref[0, i] * q_ref[1, i] * jnp.exp(-activation / theta)

    def one(s, carry):
        for i in range(planes):
            q = q_ref[s, i]
            rows, lanes = q.shape
            slope_y, near_y = slope_of(lambda k: pltpu.roll(q, (-k) % rows, 0))
            slope_z, near_z = slope_of(lambda k: pltpu.roll(q, (-k) % lanes, 1))
            smooth = dif_ref[i] * (near_y + near_z - (6.0 + mix_const) * q)
            drift = vel_ref[1, i] * slope_y + vel_ref[2, i] * slope_z
            base_ref[s, i] = q + (time_step * (smooth - drift) + stoich_ref[s] * react[i])
            noise_ref[s, i] = wie_ref[1, i] * slope_y + wie_ref[2, i] * slope_z
        return carry

    lax.fori_loop(0, scalars, one, 0)


def outer_kernel(low_hbm, high_hbm, q_ref, base_ref, noise_ref, vel_ref, wie_ref, dif_ref, base_out, noise_out, low_ref, high_ref, sems):
    scalars, planes = q_ref.shape[:2]
    cuts = [pl.ds(0, scalars // 2), pl.ds(scalars // 2, scalars // 2)]
    pairs = ((low_hbm, low_ref), (high_hbm, high_ref))
    copies = [
        [pltpu.make_async_copy(a.at[cut], b.at[cut], sems.at[m, n]) for n, (a, b) in enumerate(pairs)]
        for m, cut in enumerate(cuts)
    ]
    for copy in copies[0] + copies[1]:
        copy.start()

    def one(s, carry):
        for i in range(planes):

            def along_x(k):
                j = i + k
                if j < 0:
                    return low_ref[s, j + planes]
                if j >= planes:
                    return high_ref[s, j - planes]
                return q_ref[s, j]

            slope, near = slope_of(along_x)
            base_out[s, i] = base_ref[s, i] + time_step * (dif_ref[i] * near - vel_ref[0, i] * slope)
            noise_out[s, i] = noise_ref[s, i] + wie_ref[0, i] * slope
        return carry

    for m in range(2):
        for copy in copies[m]:
            copy.wait()
        lax.fori_loop(m * (scalars // 2), (m + 1) * (scalars // 2), one, 0)


def join_kernel(fields, last, base_ref, noise_ref, dif_ref, own_ref, other_ref, *rest):
    out_ref = rest[-1]
    scalars, planes = base_ref.shape[:2]
    half = scalars // 2
    row = lax.axis_index("field") // 8

    def total(s, i):
        return jnp.where(row == s // half, own_ref[s % half, i], other_ref[s % half, i])

    for i in range(planes):
        dif = dif_ref[i]
        theta_bar = 1.0 + 3.0 * sigmoid(total(scalars - 1, i) * (1.0 / fields))
        amplitude = jnp.sqrt(2.0 * dif * theta_bar)
        pull = (time_step * mix_const / fields) * dif
        for s in range(scalars):
            new = base_ref[s, i] + (amplitude * noise_ref[s, i] + pull * total(s, i))
            out_ref[s, i] = 0.5 * rest[0][s, i] + 0.5 * new if last else new


def spread_kernel(parts_ref, out_ref):
    total = parts_ref[0]
    for n in range(1, parts_ref.shape[0]):
        total = total + parts_ref[n]
    for n in range(out_ref.shape[0]):
        out_ref[n] = total


def section(fields, stoich, q, velocity, wiener, diffusivity, phi=None):
    last = phi is not None
    like = jax.ShapeDtypeStruct(q.shape, q.dtype)
    low, high = neighbours(q)
    base, noise = call(
        inner_kernel, (like, like), [SMEM] + [VMEM] * 4, [pltpu.VMEM(q.shape[1:], jnp.float32)], 10**6, "inner"
    )(stoich, q, velocity, wiener, diffusivity)
    mark = q
    shares = mark.reshape(lax.axis_size("field"), -1, 8, q.shape[-1])
    received = lax.all_to_all(shares, "field", 0, 0)
    spread = call(spread_kernel, jax.ShapeDtypeStruct((8,) + shares.shape[1:], q.dtype), [VMEM], [], 0, "spread")(received)
    own = lax.all_to_all(spread, "field", 0, 0, axis_index_groups=FIELD_ROWS).reshape((-1,) + q.shape[1:])
    other = lax.ppermute(own, "field", [(i, i ^ 8) for i in range(16)])
    scratch = [pltpu.VMEM(q.shape, jnp.float32)] * 2 + [pltpu.SemaphoreType.DMA((2, 2))]
    base, noise = call(outer_kernel, (like, like), [HBM] * 2 + [VMEM] * 6, scratch, 10**10, "outer", {3: 0, 4: 1})(
        low, high, q, base, noise, velocity, wiener, diffusivity
    )
    args = (base, noise, diffusivity, own, other) + ((phi,) if last else ())
    return call(functools.partial(join_kernel, fields, last), like, [VMEM] * len(args), [], 0, "join")(*args)


def neighbours(q):
    count = lax.axis_size("space")
    low = lax.ppermute(q, "space", [(i, i + 1) for i in range(count - 1)])
    high = lax.ppermute(q, "space", [(i + 1, i) for i in range(count - 1)])
    return low, high


def local(phi, velocity, wiener, diffusivity, stoich):
    fields = phi.shape[0] * lax.axis_size("field")
    phi, wiener = phi[0], wiener[0]
    first = section(fields, stoich, phi, velocity, wiener, diffusivity)
    return section(fields, stoich, first, velocity, wiener, diffusivity, phi)[None]


def solution(mesh):
    return jax.shard_map(
        local,
        mesh=mesh,
        in_specs=(
            P("field", None, "space", None, None),
            P(None, "space", None, None),
            P("field", None, "space", None, None),
            P("space", None, None),
            P(),
        ),
        out_specs=P("field", None, "space", None, None),
        check_vma=False,
    )
```

```python
import functools

import jax
import jax.numpy as jnp
from jax import lax
from jax.experimental import pallas as pl
from jax.experimental.pallas import tpu as pltpu
from jax.sharding import PartitionSpec as P

time_step = 0.3
mix_const = 5.0
pre_factor = 2.0
activation = 2.0

EARLY = 6

HBM = pl.BlockSpec(memory_space=pltpu.HBM)
SMEM = pl.BlockSpec(memory_space=pltpu.SMEM)
VMEM = pl.BlockSpec(memory_space=pltpu.VMEM)


FIELD_ROWS = [[(y * 4 + x) * 2 + c for x in range(4) for c in range(2)] for y in range(2)]
BY_X = [[(y * 4 + x) * 2 + c for x in range(4)] for y in range(2) for c in range(2)]


def call(kernel, out_shape, in_specs, scratch, flops, name, aliases={}):
    return pl.pallas_call(
        kernel,
        out_shape=out_shape,
        in_specs=in_specs,
        out_specs=jax.tree.map(lambda _: VMEM, out_shape),
        scratch_shapes=scratch,
        compiler_params=pltpu.CompilerParams(vmem_limit_bytes=16 * 2**20),
        cost_estimate=pl.CostEstimate(flops=flops, bytes_accessed=0, transcendentals=0),
        input_output_aliases=aliases,
        name=name,
    )


def sigmoid(x):
    return 1.0 / (1.0 + jnp.exp(-x))


def slope_of(at):
    up, down = at(1), at(-1)
    return 0.75 * (up - down) - 0.15 * (at(2) - at(-2)) + (1.0 / 60.0) * (at(3) - at(-3)), up + down


def inner_kernel(stoich_ref, q_ref, vel_ref, wie_ref, dif_ref, base_ref, noise_ref, react):
    scalars, planes = q_ref.shape[:2]
    for i in range(planes):
        theta = 1.0 + 3.0 * sigmoid(q_ref[scalars - 1, i])
        react[i] = (time_step * pre_factor) * q_ref[0, i] * q_ref[1, i] * jnp.exp(-activation / theta)

    def one(s, carry):
        for i in range(planes):
            q = q_ref[s, i]
            rows, lanes = q.shape
            slope_y, near_y = slope_of(lambda k: pltpu.roll(q, (-k) % rows, 0))
            slope_z, near_z = slope_of(lambda k: pltpu.roll(q, (-k) % lanes, 1))
            smooth = dif_ref[i] * (near_y + near_z - (6.0 + mix_const) * q)
            drift = vel_ref[1, i] * slope_y + vel_ref[2, i] * slope_z
            base_ref[s, i] = q + (time_step * (smooth - drift) + stoich_ref[s] * react[i])
            noise_ref[s, i] = wie_ref[1, i] * slope_y + wie_ref[2, i] * slope_z
        return carry

    lax.fori_loop(0, scalars, one, 0)


def outer_kernel(count, *refs):
    halo, (q_ref, base_ref, noise_ref, vel_ref, wie_ref, dif_ref, base_out, noise_out, low_ref, high_ref, sems) = refs[:count], refs[count:]
    scalars, planes = q_ref.shape[:2]
    edge = EARLY if count == 4 else scalars // 2
    cuts = [(0, edge), (edge, scalars)]
    copies = []
    for m, (at, end) in enumerate(cuts):
        lot = halo[2 * m : 2 * m + 2] if count == 4 else [ref.at[pl.ds(at, end - at)] for ref in halo]
        whole = [ref.at[pl.ds(at, end - at)] for ref in (low_ref, high_ref)]
        copies.append([pltpu.make_async_copy(a, b, sems.at[m, n]) for n, (a, b) in enumerate(zip(lot, whole))])
    for copy in copies[0] + copies[1]:
        copy.start()

    def one(s, carry):
        for i in range(planes):

            def along_x(k):
                j = i + k
                if j < 0:
                    return low_ref[s, j + planes]
                if j >= planes:
                    return high_ref[s, j - planes]
                return q_ref[s, j]

            slope, near = slope_of(along_x)
            base_out[s, i] = base_ref[s, i] + time_step * (dif_ref[i] * near - vel_ref[0, i] * slope)
            noise_out[s, i] = noise_ref[s, i] + wie_ref[0, i] * slope
        return carry

    for m in range(2):
        for copy in copies[m]:
            copy.wait()
        lax.fori_loop(*cuts[m], one, 0)


def join_kernel(fields, last, base_ref, noise_ref, dif_ref, *rest):
    scalars, planes = base_ref.shape[:2]
    core = lax.axis_index("field") % 2

    def total(s, i):
        if last:
            return rest[0][s, i]
        return jnp.where(core == s % 2, rest[0][s // 2, i], rest[1][s // 2, i])

    for i in range(planes):
        dif = dif_ref[i]
        theta_bar = 1.0 + 3.0 * sigmoid(total(scalars - 1, i) * (1.0 / fields))
        amplitude = jnp.sqrt(2.0 * dif * theta_bar)
        pull = (time_step * mix_const / fields) * dif
        for s in range(scalars):
            new = base_ref[s, i] + (amplitude * noise_ref[s, i] + pull * total(s, i))
            rest[2][s, i] = 0.5 * rest[1][s, i] + 0.5 * new if last else new


def spread_kernel(parts_ref, out_ref):
    total = parts_ref[0]
    for n in range(1, parts_ref.shape[0]):
        total = total + parts_ref[n]
    for n in range(out_ref.shape[0]):
        out_ref[n] = total


def add_kernel(a_ref, b_ref, out_ref):
    for n in range(out_ref.shape[0]):
        out_ref[n] = a_ref[n] + b_ref[n]


def flip(a, bit):
    return lax.ppermute(a, "field", [(i, i ^ bit) for i in range(16)])


def section(fields, stoich, q, velocity, wiener, diffusivity, phi=None):
    last = phi is not None
    scalars = q.shape[0]
    like = lambda *lead: jax.ShapeDtypeStruct(lead + q.shape[1:], q.dtype)
    halo = neighbours(q if last else q[:EARLY])
    base, noise = call(
        inner_kernel, (like(scalars),) * 2, [SMEM] + [VMEM] * 4, [pltpu.VMEM(q.shape[1:], jnp.float32)], 10**6, "inner"
    )(stoich, q, velocity, wiener, diffusivity)
    if last:
        shares = q.reshape(lax.axis_size("field"), -1, 8, q.shape[-1])
        received = lax.all_to_all(shares, "field", 0, 0)
        spread = call(spread_kernel, jax.ShapeDtypeStruct(shares.shape, q.dtype), [VMEM], [], 0, "spread")(received)
        totals = (lax.all_to_all(spread, "field", 0, 0).reshape(q.shape),)
    else:
        received = lax.all_to_all(q, "field", 0, 0, axis_index_groups=FIELD_ROWS)
        spread = call(spread_kernel, like(4), [VMEM], [], 0, "spread")(received)
        part = lax.all_to_all(spread, "field", 0, 0, axis_index_groups=BY_X)
        part, late = lax.optimization_barrier((part, q[EARLY:]))
        own = call(add_kernel, like(4), [VMEM] * 2, [], 0, "add")(part, flip(part, 8))
        halo += neighbours(late)
        totals = (own, flip(own, 1))
    scratch = [pltpu.VMEM(q.shape, jnp.float32)] * 2 + [pltpu.SemaphoreType.DMA((2, 2))]
    count = len(halo)
    base, noise = call(
        functools.partial(outer_kernel, count),
        (like(scalars),) * 2,
        [HBM] * count + [VMEM] * 6,
        scratch,
        10**10,
        "outer",
        {count + 1: 0, count + 2: 1},
    )(*halo, q, base, noise, velocity, wiener, diffusivity)
    args = (base, noise, diffusivity) + totals + ((phi,) if last else ())
    return call(functools.partial(join_kernel, fields, last), like(scalars), [VMEM] * len(args), [], 0, "join")(*args)


def neighbours(q):
    count = lax.axis_size("space")
    low = lax.ppermute(q, "space", [(i, i + 1) for i in range(count - 1)])
    high = lax.ppermute(q, "space", [(i + 1, i) for i in range(count - 1)])
    return low, high


def local(phi, velocity, wiener, diffusivity, stoich):
    fields = phi.shape[0] * lax.axis_size("field")
    phi, wiener = phi[0], wiener[0]
    first = section(fields, stoich, phi, velocity, wiener, diffusivity)
    return section(fields, stoich, first, velocity, wiener, diffusivity, phi)[None]


def solution(mesh):
    return jax.shard_map(
        local,
        mesh=mesh,
        in_specs=(
            P("field", None, "space", None, None),
            P(None, "space", None, None),
            P("field", None, "space", None, None),
            P("space", None, None),
            P(),
        ),
        out_specs=P("field", None, "space", None, None),
        check_vma=False,
    )
```

```python
import functools

import jax
import jax.numpy as jnp
from jax import lax
from jax.experimental import pallas as pl
from jax.experimental.pallas import tpu as pltpu
from jax.sharding import PartitionSpec as P

time_step = 0.3
mix_const = 5.0
pre_factor = 2.0
activation = 2.0

HBM = pl.BlockSpec(memory_space=pltpu.HBM)
SMEM = pl.BlockSpec(memory_space=pltpu.SMEM)
VMEM = pl.BlockSpec(memory_space=pltpu.VMEM)


def call(kernel, out_shape, in_specs, scratch, flops, name, aliases={}):
    return pl.pallas_call(
        kernel,
        out_shape=out_shape,
        in_specs=in_specs,
        out_specs=jax.tree.map(lambda _: VMEM, out_shape),
        scratch_shapes=scratch,
        compiler_params=pltpu.CompilerParams(vmem_limit_bytes=16 * 2**20),
        cost_estimate=pl.CostEstimate(flops=flops, bytes_accessed=0, transcendentals=0),
        input_output_aliases=aliases,
        name=name,
    )


def sigmoid(x):
    return 1.0 / (1.0 + jnp.exp(-x))


def slope_of(at):
    up, down = at(1), at(-1)
    return 0.75 * (up - down) - 0.15 * (at(2) - at(-2)) + (1.0 / 60.0) * (at(3) - at(-3)), up + down


def inner_kernel(stoich_ref, q_ref, vel_ref, wie_ref, dif_ref, base_ref, noise_ref, react):
    scalars, planes = q_ref.shape[:2]
    for i in range(planes):
        theta = 1.0 + 3.0 * sigmoid(q_ref[scalars - 1, i])
        react[i] = (time_step * pre_factor) * q_ref[0, i] * q_ref[1, i] * jnp.exp(-activation / theta)

    def one(s, carry):
        for i in range(planes):
            q = q_ref[s, i]
            rows, lanes = q.shape
            slope_y, near_y = slope_of(lambda k: pltpu.roll(q, (-k) % rows, 0))
            slope_z, near_z = slope_of(lambda k: pltpu.roll(q, (-k) % lanes, 1))
            smooth = dif_ref[i] * (near_y + near_z - (6.0 + mix_const) * q)
            drift = vel_ref[1, i] * slope_y + vel_ref[2, i] * slope_z
            base_ref[s, i] = q + (time_step * (smooth - drift) + stoich_ref[s] * react[i])
            noise_ref[s, i] = wie_ref[1, i] * slope_y + wie_ref[2, i] * slope_z
        return carry

    lax.fori_loop(0, scalars, one, 0)


def outer_kernel(first_hbm, second_hbm, q_ref, base_ref, noise_ref, vel_ref, wie_ref, dif_ref, base_out, noise_out, halo_ref, sems):
    scalars, planes = q_ref.shape[:2]
    cuts = [pl.ds(0, scalars // 2), pl.ds(scalars // 2, scalars // 2)]
    odd = lax.axis_index("space") % 2
    low_ref, high_ref = halo_ref.at[0], halo_ref.at[1]
    pairs = ((first_hbm, halo_ref.at[1 - odd]), (second_hbm, halo_ref.at[odd]))
    copies = [
        [pltpu.make_async_copy(a.at[cut], b.at[cut], sems.at[m, n]) for n, (a, b) in enumerate(pairs)]
        for m, cut in enumerate(cuts)
    ]
    for copy in copies[0] + copies[1]:
        copy.start()

    def one(s, carry):
        for i in range(planes):

            def along_x(k):
                j = i + k
                if j < 0:
                    return low_ref[s, j + planes]
                if j >= planes:
                    return high_ref[s, j - planes]
                return q_ref[s, j]

            slope, near = slope_of(along_x)
            base_out[s, i] = base_ref[s, i] + time_step * (dif_ref[i] * near - vel_ref[0, i] * slope)
            noise_out[s, i] = noise_ref[s, i] + wie_ref[0, i] * slope
        return carry

    for m in range(2):
        for copy in copies[m]:
            copy.wait()
        lax.fori_loop(m * (scalars // 2), (m + 1) * (scalars // 2), one, 0)


def join_kernel(fields, last, base_ref, noise_ref, dif_ref, total_ref, *rest):
    out_ref = rest[-1]
    scalars, planes = base_ref.shape[:2]
    for i in range(planes):
        dif = dif_ref[i]
        theta_bar = 1.0 + 3.0 * sigmoid(total_ref[scalars - 1, i] * (1.0 / fields))
        amplitude = jnp.sqrt(2.0 * dif * theta_bar)
        pull = (time_step * mix_const / fields) * dif
        for s in range(scalars):
            new = base_ref[s, i] + (amplitude * noise_ref[s, i] + pull * total_ref[s, i])
            out_ref[s, i] = 0.5 * rest[0][s, i] + 0.5 * new if last else new


def spread_kernel(parts_ref, out_ref):
    total = parts_ref[0]
    for n in range(1, parts_ref.shape[0]):
        total = total + parts_ref[n]
    for n in range(out_ref.shape[0]):
        out_ref[n] = total


def section(fields, stoich, q, velocity, wiener, diffusivity, phi=None):
    last = phi is not None
    like = jax.ShapeDtypeStruct(q.shape, q.dtype)
    halo = neighbours(q)
    base, noise = call(
        inner_kernel, (like, like), [SMEM] + [VMEM] * 4, [pltpu.VMEM(q.shape[1:], jnp.float32)], 10**6, "inner"
    )(stoich, q, velocity, wiener, diffusivity)
    mark = q
    shares = mark.reshape(lax.axis_size("field"), -1, 8, q.shape[-1])
    received = lax.all_to_all(shares, "field", 0, 0)
    spread = call(spread_kernel, jax.ShapeDtypeStruct(shares.shape, q.dtype), [VMEM], [], 0, "spread")(received)
    total = lax.all_to_all(spread, "field", 0, 0).reshape(q.shape)
    scratch = [pltpu.VMEM((2,) + q.shape, jnp.float32)] + [pltpu.SemaphoreType.DMA((2, 2))]
    base, noise = call(outer_kernel, (like, like), [HBM] * 2 + [VMEM] * 6, scratch, 10**10, "outer", {3: 0, 4: 1})(
        *halo, q, base, noise, velocity, wiener, diffusivity
    )
    args = (base, noise, diffusivity, total) + ((phi,) if last else ())
    return call(functools.partial(join_kernel, fields, last), like, [VMEM] * len(args), [], 0, "join")(*args)


def neighbours(q):
    count = lax.axis_size("space")
    swaps = [[(i, i + 1) for i in range(begin, count - 1, 2)] for begin in range(2)]
    return tuple(lax.ppermute(q, "space", pairs + [(b, a) for a, b in pairs]) for pairs in swaps)


def local(phi, velocity, wiener, diffusivity, stoich):
    fields = phi.shape[0] * lax.axis_size("field")
    phi, wiener = phi[0], wiener[0]
    first = section(fields, stoich, phi, velocity, wiener, diffusivity)
    return section(fields, stoich, first, velocity, wiener, diffusivity, phi)[None]


def solution(mesh):
    return jax.shard_map(
        local,
        mesh=mesh,
        in_specs=(
            P("field", None, "space", None, None),
            P(None, "space", None, None),
            P("field", None, "space", None, None),
            P("space", None, None),
            P(),
        ),
        out_specs=P("field", None, "space", None, None),
        check_vma=False,
    )
```

```python
import functools

import jax
import jax.numpy as jnp
from jax import lax
from jax.experimental import pallas as pl
from jax.experimental.pallas import tpu as pltpu
from jax.sharding import PartitionSpec as P

time_step = 0.3
mix_const = 5.0
pre_factor = 2.0
activation = 2.0

HBM = pl.BlockSpec(memory_space=pltpu.HBM)
SMEM = pl.BlockSpec(memory_space=pltpu.SMEM)
VMEM = pl.BlockSpec(memory_space=pltpu.VMEM)


def call(kernel, out_shape, in_specs, scratch, flops, name, aliases={}):
    return pl.pallas_call(
        kernel,
        out_shape=out_shape,
        in_specs=in_specs,
        out_specs=jax.tree.map(lambda _: VMEM, out_shape),
        scratch_shapes=scratch,
        compiler_params=pltpu.CompilerParams(vmem_limit_bytes=16 * 2**20),
        cost_estimate=pl.CostEstimate(flops=flops, bytes_accessed=0, transcendentals=0),
        input_output_aliases=aliases,
        name=name,
    )


def sigmoid(x):
    return 1.0 / (1.0 + jnp.exp(-x))


def slope_of(at):
    up, down = at(1), at(-1)
    return 0.75 * (up - down) - 0.15 * (at(2) - at(-2)) + (1.0 / 60.0) * (at(3) - at(-3)), up + down


def inner_kernel(stoich_ref, q_ref, vel_ref, wie_ref, dif_ref, base_ref, noise_ref, react):
    scalars, planes = q_ref.shape[:2]
    for i in range(planes):
        theta = 1.0 + 3.0 * sigmoid(q_ref[scalars - 1, i])
        react[i] = (time_step * pre_factor) * q_ref[0, i] * q_ref[1, i] * jnp.exp(-activation / theta)

    def one(s, carry):
        for i in range(planes):
            q = q_ref[s, i]
            rows, lanes = q.shape
            slope_y, near_y = slope_of(lambda k: pltpu.roll(q, (-k) % rows, 0))
            slope_z, near_z = slope_of(lambda k: pltpu.roll(q, (-k) % lanes, 1))
            smooth = dif_ref[i] * (near_y + near_z - (6.0 + mix_const) * q)
            drift = vel_ref[1, i] * slope_y + vel_ref[2, i] * slope_z
            base_ref[s, i] = q + (time_step * (smooth - drift) + stoich_ref[s] * react[i])
            noise_ref[s, i] = wie_ref[1, i] * slope_y + wie_ref[2, i] * slope_z
        return carry

    lax.fori_loop(0, scalars, one, 0)


def outer_kernel(first_hbm, second_hbm, q_ref, base_ref, noise_ref, vel_ref, wie_ref, dif_ref, base_out, noise_out, halo_ref, sems):
    scalars, planes = q_ref.shape[:2]
    cuts = [pl.ds(0, scalars // 2), pl.ds(scalars // 2, scalars // 2)]
    odd = (lax.axis_index("space") + lax.axis_index("field")) % 2
    low_ref, high_ref = halo_ref.at[0], halo_ref.at[1]
    pairs = ((first_hbm, halo_ref.at[1 - odd]), (second_hbm, halo_ref.at[odd]))
    copies = [
        [pltpu.make_async_copy(a.at[cut], b.at[cut], sems.at[m, n]) for n, (a, b) in enumerate(pairs)]
        for m, cut in enumerate(cuts)
    ]
    for copy in copies[0] + copies[1]:
        copy.start()

    def one(s, carry):
        for i in range(planes):

            def along_x(k):
                j = i + k
                if j < 0:
                    return low_ref[s, j + planes]
                if j >= planes:
                    return high_ref[s, j - planes]
                return q_ref[s, j]

            slope, near = slope_of(along_x)
            base_out[s, i] = base_ref[s, i] + time_step * (dif_ref[i] * near - vel_ref[0, i] * slope)
            noise_out[s, i] = noise_ref[s, i] + wie_ref[0, i] * slope
        return carry

    for m in range(2):
        for copy in copies[m]:
            copy.wait()
        lax.fori_loop(m * (scalars // 2), (m + 1) * (scalars // 2), one, 0)


def join_kernel(fields, last, base_ref, noise_ref, dif_ref, total_ref, *rest):
    out_ref = rest[-1]
    scalars, planes = base_ref.shape[:2]
    for i in range(planes):
        dif = dif_ref[i]
        theta_bar = 1.0 + 3.0 * sigmoid(total_ref[scalars - 1, i] * (1.0 / fields))
        amplitude = jnp.sqrt(2.0 * dif * theta_bar)
        pull = (time_step * mix_const / fields) * dif
        for s in range(scalars):
            new = base_ref[s, i] + (amplitude * noise_ref[s, i] + pull * total_ref[s, i])
            out_ref[s, i] = 0.5 * rest[0][s, i] + 0.5 * new if last else new


def spread_kernel(parts_ref, out_ref):
    total = parts_ref[0]
    for n in range(1, parts_ref.shape[0]):
        total = total + parts_ref[n]
    for n in range(out_ref.shape[0]):
        out_ref[n] = total


def section(fields, stoich, q, velocity, wiener, diffusivity, phi=None):
    last = phi is not None
    like = jax.ShapeDtypeStruct(q.shape, q.dtype)
    halo = neighbours(q)
    base, noise = call(
        inner_kernel, (like, like), [SMEM] + [VMEM] * 4, [pltpu.VMEM(q.shape[1:], jnp.float32)], 10**6, "inner"
    )(stoich, q, velocity, wiener, diffusivity)
    mark = q
    shares = mark.reshape(lax.axis_size("field"), -1, 8, q.shape[-1])
    received = lax.all_to_all(shares, "field", 0, 0)
    spread = call(spread_kernel, jax.ShapeDtypeStruct(shares.shape, q.dtype), [VMEM], [], 0, "spread")(received)
    total = lax.all_to_all(spread, "field", 0, 0).reshape(q.shape)
    scratch = [pltpu.VMEM((2,) + q.shape, jnp.float32)] + [pltpu.SemaphoreType.DMA((2, 2))]
    base, noise = call(outer_kernel, (like, like), [HBM] * 2 + [VMEM] * 6, scratch, 10**10, "outer", {3: 0, 4: 1})(
        *halo, q, base, noise, velocity, wiener, diffusivity
    )
    args = (base, noise, diffusivity, total) + ((phi,) if last else ())
    return call(functools.partial(join_kernel, fields, last), like, [VMEM] * len(args), [], 0, "join")(*args)


def neighbours(q):
    count, fields = lax.axis_size("space"), lax.axis_size("field")

    def swap(n):
        ones = [(i, f) for f in range(fields) for i in range((n + f) % 2, count - 1, 2)]
        pairs = [(i * fields + f, (i + 1) * fields + f) for i, f in ones]
        return lax.ppermute(q, ("space", "field"), pairs + [(b, a) for a, b in pairs])

    return swap(0), swap(1)


def local(phi, velocity, wiener, diffusivity, stoich):
    fields = phi.shape[0] * lax.axis_size("field")
    phi, wiener = phi[0], wiener[0]
    first = section(fields, stoich, phi, velocity, wiener, diffusivity)
    return section(fields, stoich, first, velocity, wiener, diffusivity, phi)[None]


def solution(mesh):
    return jax.shard_map(
        local,
        mesh=mesh,
        in_specs=(
            P("field", None, "space", None, None),
            P(None, "space", None, None),
            P("field", None, "space", None, None),
            P("space", None, None),
            P(),
        ),
        out_specs=P("field", None, "space", None, None),
        check_vma=False,
    )
```

```python
import functools

import jax
import jax.numpy as jnp
from jax import lax
from jax.experimental import pallas as pl
from jax.experimental.pallas import tpu as pltpu
from jax.sharding import PartitionSpec as P

time_step = 0.3
mix_const = 5.0
pre_factor = 2.0
activation = 2.0

HBM = pl.BlockSpec(memory_space=pltpu.HBM)
SMEM = pl.BlockSpec(memory_space=pltpu.SMEM)
VMEM = pl.BlockSpec(memory_space=pltpu.VMEM)


def call(kernel, out_shape, in_specs, scratch, flops, name, aliases={}):
    return pl.pallas_call(
        kernel,
        out_shape=out_shape,
        in_specs=in_specs,
        out_specs=jax.tree.map(lambda _: VMEM, out_shape),
        scratch_shapes=scratch,
        compiler_params=pltpu.CompilerParams(vmem_limit_bytes=16 * 2**20),
        cost_estimate=pl.CostEstimate(flops=flops, bytes_accessed=0, transcendentals=0),
        input_output_aliases=aliases,
        name=name,
    )


def sigmoid(x):
    return 1.0 / (1.0 + jnp.exp(-x))


def slope_of(at):
    up, down = at(1), at(-1)
    return 0.75 * (up - down) - 0.15 * (at(2) - at(-2)) + (1.0 / 60.0) * (at(3) - at(-3)), up + down


def inner_kernel(stoich_ref, q_ref, vel_ref, wie_ref, dif_ref, base_ref, noise_ref, react):
    scalars, planes = q_ref.shape[:2]
    for i in range(planes):
        theta = 1.0 + 3.0 * sigmoid(q_ref[scalars - 1, i])
        react[i] = (time_step * pre_factor) * q_ref[0, i] * q_ref[1, i] * jnp.exp(-activation / theta)

    def one(s, carry):
        for i in range(planes):
            q = q_ref[s, i]
            rows, lanes = q.shape
            slope_y, near_y = slope_of(lambda k: pltpu.roll(q, (-k) % rows, 0))
            slope_z, near_z = slope_of(lambda k: pltpu.roll(q, (-k) % lanes, 1))
            smooth = dif_ref[i] * (near_y + near_z - (6.0 + mix_const) * q)
            drift = vel_ref[1, i] * slope_y + vel_ref[2, i] * slope_z
            base_ref[s, i] = q + (time_step * (smooth - drift) + stoich_ref[s] * react[i])
            noise_ref[s, i] = wie_ref[1, i] * slope_y + wie_ref[2, i] * slope_z
        return carry

    lax.fori_loop(0, scalars, one, 0)


def outer_kernel(first_hbm, second_hbm, q_ref, base_ref, noise_ref, vel_ref, wie_ref, dif_ref, base_out, noise_out, halo_ref, sems):
    scalars, planes = q_ref.shape[:2]
    cuts = [pl.ds(0, scalars // 2), pl.ds(scalars // 2, scalars // 2)]
    odd = (lax.axis_index("space") + lax.axis_index("field")) % 2
    low_ref, high_ref = halo_ref.at[0], halo_ref.at[1]
    pairs = ((first_hbm, halo_ref.at[1 - odd]), (second_hbm, halo_ref.at[odd]))
    copies = [
        [pltpu.make_async_copy(a.at[cut], b.at[cut], sems.at[m, n]) for n, (a, b) in enumerate(pairs)]
        for m, cut in enumerate(cuts)
    ]
    for copy in copies[0] + copies[1]:
        copy.start()

    def one(s, carry):
        for i in range(planes):

            def along_x(k):
                j = i + k
                if j < 0:
                    return low_ref[s, j + planes]
                if j >= planes:
                    return high_ref[s, j - planes]
                return q_ref[s, j]

            slope, near = slope_of(along_x)
            base_out[s, i] = base_ref[s, i] + time_step * (dif_ref[i] * near - vel_ref[0, i] * slope)
            noise_out[s, i] = noise_ref[s, i] + wie_ref[0, i] * slope
        return carry

    for m in range(2):
        for copy in copies[m]:
            copy.wait()
        lax.fori_loop(m * (scalars // 2), (m + 1) * (scalars // 2), one, 0)


def join_kernel(fields, last, base_ref, noise_ref, dif_ref, total_ref, *rest):
    out_ref = rest[-1]
    scalars, planes = base_ref.shape[:2]
    for i in range(planes):
        dif = dif_ref[i]
        theta_bar = 1.0 + 3.0 * sigmoid(total_ref[scalars - 1, i] * (1.0 / fields))
        amplitude = jnp.sqrt(2.0 * dif * theta_bar)
        pull = (time_step * mix_const / fields) * dif
        for s in range(scalars):
            new = base_ref[s, i] + (amplitude * noise_ref[s, i] + pull * total_ref[s, i])
            out_ref[s, i] = 0.5 * rest[0][s, i] + 0.5 * new if last else new


def spread_kernel(parts_ref, out_ref):
    total = parts_ref[0]
    for n in range(1, parts_ref.shape[0]):
        total = total + parts_ref[n]
    for n in range(out_ref.shape[0]):
        out_ref[n] = total


def section(fields, stoich, q, velocity, wiener, diffusivity, phi=None):
    last = phi is not None
    like = jax.ShapeDtypeStruct(q.shape, q.dtype)
    halo = neighbours(q)
    base, noise = call(
        inner_kernel, (like, like), [SMEM] + [VMEM] * 4, [pltpu.VMEM(q.shape[1:], jnp.float32)], 10**6, "inner"
    )(stoich, q, velocity, wiener, diffusivity)
    mark = q
    shares = mark.reshape(lax.axis_size("field"), -1, 8, q.shape[-1])
    received = lax.all_to_all(shares, "field", 0, 0)
    spread = call(spread_kernel, jax.ShapeDtypeStruct(shares.shape, q.dtype), [VMEM], [], 0, "spread")(received)
    total = lax.all_to_all(spread, "field", 0, 0).reshape(q.shape)
    scratch = [pltpu.VMEM((2,) + q.shape, jnp.float32)] + [pltpu.SemaphoreType.DMA((2, 2))]
    base, noise = call(outer_kernel, (like, like), [HBM] * 2 + [VMEM] * 6, scratch, 2 * 10**10, "outer", {3: 0, 4: 1})(
        *halo, q, base, noise, velocity, wiener, diffusivity
    )
    args = (base, noise, diffusivity, total) + ((phi,) if last else ())
    return call(functools.partial(join_kernel, fields, last), like, [VMEM] * len(args), [], 0, "join")(*args)


def neighbours(q):
    count, fields = lax.axis_size("space"), lax.axis_size("field")

    def swap(n):
        ones = [(i, f) for f in range(fields) for i in range((n + f) % 2, count - 1, 2)]
        pairs = [(i * fields + f, (i + 1) * fields + f) for i, f in ones]
        return lax.ppermute(q, ("space", "field"), pairs + [(b, a) for a, b in pairs])

    return swap(0), swap(1)


def local(phi, velocity, wiener, diffusivity, stoich):
    fields = phi.shape[0] * lax.axis_size("field")
    phi, wiener = phi[0], wiener[0]
    first = section(fields, stoich, phi, velocity, wiener, diffusivity)
    return section(fields, stoich, first, velocity, wiener, diffusivity, phi)[None]


def solution(mesh):
    return jax.shard_map(
        local,
        mesh=mesh,
        in_specs=(
            P("field", None, "space", None, None),
            P(None, "space", None, None),
            P("field", None, "space", None, None),
            P("space", None, None),
            P(),
        ),
        out_specs=P("field", None, "space", None, None),
        check_vma=False,
    )
```
